128 devices in a mesh: row: 16 (over z, y), col: 8 (over x, core).
Axes of the slice: x: 4, y: 4, z: 4, core: 2. Of those that a mesh axis runs over, the one named last changes fastest.
Arguments:
- matrix: bfloat16 [28672, 28672], P('row', 'col'), may hold values from -1.5 to 16, as said below
Outputs:
- factored: bfloat16 [28672, 28672], P('row', 'col')
The draws below stay inside these ranges and needn't reach their ends.
Inputs may be any that keep to these rules, and one draw needn't show every extreme that they name: `matrix`: in logical order, diagonal entries lie between 12 and 16 and off-diagonal entries have magnitude at most 1.5.
All inputs are finite; a program needn't handle non-finite values.
Results may differ from the reference program's by a relative error of at most 0.0025.
The reference program's roundings to bfloat16 on the way count: a program that leaves them out, or rounds other values in their place, can miss the bound.
Values may be sent and summed in bfloat16 or wider, within the bound.
A program may use at most 192 MiB of HBM per device.

```python
import jax
import jax.numpy as jnp
from jax import lax

N = 28672
NB = 256
STEPS = 2
N_ROW = 16
N_COL = 8


def draw_matrix(key, part):
    key_off = jax.random.fold_in(key, 11)
    key_diag = jax.random.fold_in(key, 12)
    key_front = jax.random.fold_in(key, 13)
    off_diag = jnp.clip(jax.random.normal(key_off, (N, N), jnp.float32) * 0.25, -1.5, 1.5)
    diag_values = jax.random.uniform(key_diag, (N,), jnp.float32, 12.0, 16.0)
    front_values = jax.random.uniform(key_front, (N, N), jnp.float32, 0.0, 1.5)
    stored = jnp.arange(N, dtype=jnp.int32)
    row_len = N // N_ROW
    col_len = N // N_COL
    row_logical = (stored % row_len // NB * N_ROW + stored // row_len) * NB + stored % NB
    col_logical = (stored % col_len // NB * N_COL + stored // col_len) * NB + stored % NB
    row_panel = row_logical // NB
    col_panel = col_logical // NB
    in_front = (row_panel[:, None] == col_panel[None, :]) & (row_panel[:, None] < STEPS)
    off_diag = jnp.where(in_front, front_values, off_diag)
    full = jnp.where(row_logical[:, None] == col_logical[None, :], diag_values[row_logical][:, None], off_diag)
    return full.astype(jnp.bfloat16)


def setup_inputs(seed: int = 0) -> dict:
    key_of = jax.random.split(jax.random.key(seed), 2)
    matrix = draw_matrix(jax.random.fold_in(key_of[1], 71), 0)
    return dict(matrix=matrix)


def factor_block(block):
    work = block.astype(jnp.float32)
    size = work.shape[0]
    positions = jnp.arange(size, dtype=jnp.int32)

    def eliminate(column, work):
        values = lax.dynamic_slice_in_dim(work, column, 1, 1)[:, 0]
        pivot_row = lax.dynamic_slice_in_dim(work, column, 1, 0)[0]
        pivot = jnp.sum(jnp.where(positions == column, pivot_row, 0.0))
        scaled = jnp.where(positions > column, values / pivot, 0.0)
        across = jnp.where(positions > column, pivot_row, 0.0)
        work = work - scaled[:, None] * across[None, :]
        kept = jnp.where(positions > column, scaled, values)
        return jnp.where(positions[None, :] == column, kept[:, None], work)

    return lax.fori_loop(0, size, eliminate, work)


def invert_upper(upper):
    size = upper.shape[0]
    positions = jnp.arange(size, dtype=jnp.int32)

    def substitute(count, inverse):
        index = (size - 1 - count)
        line = lax.dynamic_slice_in_dim(upper, index, 1, 0)[0]
        strict = jnp.where(positions > index, line, 0.0)
        pivot = jnp.sum(jnp.where(positions == index, line, 0.0))
        unit = jnp.where(positions == index, 1.0, 0.0).astype(jnp.float32)
        fresh = (unit - jnp.dot(strict, inverse, precision=lax.Precision.HIGHEST)) / pivot
        return jnp.where(positions[:, None] == index, fresh[None, :], inverse)

    return lax.fori_loop(0, size, substitute, jnp.zeros((size, size), jnp.float32))


def invert_lower(lower):
    size = lower.shape[0]
    positions = jnp.arange(size, dtype=jnp.int32)

    def substitute(index, inverse):
        line = lax.dynamic_slice_in_dim(lower, index, 1, 0)[0]
        strict = jnp.where(positions < index, line, 0.0)
        unit = jnp.where(positions == index, 1.0, 0.0).astype(jnp.float32)
        fresh = unit - jnp.dot(strict, inverse, precision=lax.Precision.HIGHEST)
        return jnp.where(positions[:, None] == index, fresh[None, :], inverse)

    return lax.fori_loop(0, size, substitute, jnp.zeros((size, size), jnp.float32))


def to_logical(stored):
    shaped = stored.reshape(N_ROW, N // N_ROW // NB, NB, N_COL, N // N_COL // NB, NB)
    return shaped.transpose(1, 0, 2, 4, 3, 5).reshape(N, N)


def to_stored(logical):
    shaped = logical.reshape(N // N_ROW // NB, N_ROW, NB, N // N_COL // NB, N_COL, NB)
    return shaped.transpose(1, 0, 2, 4, 3, 5).reshape(N, N)


def reference(matrix):
    work = to_logical(matrix)
    for section in range(STEPS):
        start = section * NB
        finish = start + NB
        packed = factor_block(work[start:finish, start:finish])
        upper = jnp.triu(packed)
        lower = jnp.tril(packed, -1) + jnp.eye(NB, dtype=packed.dtype)
        upper_inverse = invert_upper(upper)
        lower_inverse = invert_lower(lower)
        below = work[finish:, start:finish].astype(jnp.float32)
        left_panel = jnp.dot(below, upper_inverse, precision=lax.Precision.HIGHEST).astype(jnp.bfloat16)
        right = work[start:finish, finish:].astype(jnp.float32)
        top_panel = jnp.dot(lower_inverse, right, precision=lax.Precision.HIGHEST).astype(jnp.bfloat16)
        pieces = []
        for first in range(finish, N, 4096):
            last = min(first + 4096, N)
            update = jnp.dot(left_panel[first - finish:last - finish], top_panel, preferred_element_type=jnp.float32)
            pieces.append((work[first:last, finish:].astype(jnp.float32) - update).astype(jnp.bfloat16))
        work = work.at[start:finish, start:finish].set(packed.astype(jnp.bfloat16))
        work = work.at[finish:, start:finish].set(left_panel)
        work = work.at[start:finish, finish:].set(top_panel)
        work = work.at[finish:, finish:].set(jnp.concatenate(pieces, axis=0))
    return to_stored(work)
```

```python
import functools
import jax, jax.numpy as jnp
from jax import lax
from jax.experimental import pallas as pl
from jax.experimental.pallas import tpu as pltpu
from jax.sharding import PartitionSpec as P
NB=256
F=jnp.float32
BF=jnp.bfloat16

def split2(x):
    hi=x.astype(BF); lo=(x-hi.astype(F)).astype(BF)
    return hi,lo
def dotT(a,b):
    return lax.dot_general(a,b,(((1,),(1,)),((),())),preferred_element_type=F)

def sub_bcast(x,i):
    return jnp.broadcast_to(x[i:i+1,:],(8,128))

def recip(p):
    r=pl.reciprocal(p,approx=True)
    r=r*(2.0-p*r)
    r=r*(2.0-p*r)
    return r

def panel(q, PR, PT, sub, lane):
    base=(q%4)*32
    hi=(q>=4)
    E=[jnp.where(lane==base+8*g+sub,1.0,0.0).astype(F) for g in range(4)]
    E2=list(E)
    rpv=[jnp.zeros((8,128),F) for _ in range(4)]
    for s in range(4):
        idx=[jnp.full((8,128),base+8*s+m,jnp.int32) for m in range(8)]
        R=[[None]*4 for _ in range(8)]; Q=[[None]*4 for _ in range(8)]
        for g in range(s,4):
            tr=jnp.where(hi,PR[g][1],PR[g][0]); tt=jnp.where(hi,PT[g][1],PT[g][0])
            for m in range(8):
                R[m][g]=jnp.take_along_axis(tr,idx[m],axis=1,mode="promise_in_bounds")
                Q[m][g]=jnp.take_along_axis(tt,idx[m],axis=1,mode="promise_in_bounds")
        for i in range(8):
            rp=recip(sub_bcast(R[i][s],i))
            rpv[s]=jnp.where(sub==i,rp,rpv[s])
            pr=[sub_bcast(PR[s][h],i) for h in range(2)]+[sub_bcast(E[s],i)]
            pt=[sub_bcast(PT[s][h],i) for h in range(2)]+[sub_bcast(E2[s],i)]
            rb={m:sub_bcast(R[m][s],i) for m in range(i+1,8)}
            qb={m:sub_bcast(Q[m][s],i) for m in range(i+1,8)}
            for g in range(s,4):
                l=R[i][g]*rp; u=Q[i][g]*rp
                if g==s:
                    if i==7: continue
                    l=jnp.where(sub>i,l,0.0); u=jnp.where(sub>i,u,0.0)
                for m in range(i+1,8):
                    R[m][g]=R[m][g]-l*rb[m]
                    Q[m][g]=Q[m][g]-u*qb[m]
                for h in range(2):
                    PR[g][h]=PR[g][h]-l*pr[h]
                    PT[g][h]=PT[g][h]-u*pt[h]
                E[g]=E[g]-l*pr[2]
                E2[g]=E2[g]-u*pt[2]
    return PR,PT,E,E2,rpv

def rank_update(ref, XT, Y, inp):
    xh,xl=split2(XT); yh,yl=split2(Y)
    X=jnp.concatenate([xh,xh,xl],axis=0)
    Y3=jnp.concatenate([yh,yl,yh],axis=0)
    up=lax.dot_general(X,Y3,(((0,),(0,)),((),())),preferred_element_type=F)
    ref[...]=jnp.where(inp,0.0,ref[...])-up

def lu_inv(a_bf, W, V, U, LT, LI, UT, hooks=()):
    r0=lax.broadcasted_iota(jnp.int32,(256,256),0); c0=lax.broadcasted_iota(jnp.int32,(256,256),1)
    eye=jnp.where(r0==c0,1.0,0.0).astype(BF)
    W[...]=a_bf.astype(F)
    V[...]=dotT(eye,a_bf)
    sub=lax.broadcasted_iota(jnp.int32,(8,128),0); lane=lax.broadcasted_iota(jnp.int32,(8,128),1)
    def body(q,_):
        for at, hook in hooks:
            pl.when(q==at)(hook)
        o=pl.multiple_of(q*32,32)
        PR=[[W[pl.ds(o+8*g,8),128*h:128*h+128] for h in range(2)] for g in range(4)]
        PT=[[V[pl.ds(o+8*g,8),128*h:128*h+128] for h in range(2)] for g in range(4)]
        PR,PT,E,E2,rpv=panel(q,PR,PT,sub,lane)
        XL=[];XU=[];YR=[];YT=[]
        for g in range(4):
            a=[];b=[];c=[];d=[]
            for h in range(2):
                gl=lane+128*h
                inp=(gl>=o)&(gl<o+32); right=gl>=o+32; left=gl<o
                ur=PR[g][h]; ut=PT[g][h]
                lt=ut*rpv[g]; un=ur*rpv[g]
                U[pl.ds(o+8*g,8),128*h:128*h+128]=ur
                LT[pl.ds(o+8*g,8),128*h:128*h+128]=lt
                mr=jnp.where(inp,E[g],ur); mt=jnp.where(inp,E2[g],ut)
                LI[pl.ds(o+8*g,8),128*h:128*h+128]=jnp.where(right,0.0,mr)
                UT[pl.ds(o+8*g,8),128*h:128*h+128]=jnp.where(right,0.0,mt*rpv[g])
                a.append(jnp.where(right,lt,0.0)); b.append(jnp.where(right,un,0.0)); c.append(mr); d.append(mt)
            XL.append(jnp.concatenate(a,1)); XU.append(jnp.concatenate(b,1)); YR.append(jnp.concatenate(c,1)); YT.append(jnp.concatenate(d,1))
        XL=jnp.concatenate(XL,0);XU=jnp.concatenate(XU,0);YR=jnp.concatenate(YR,0);YT=jnp.concatenate(YT,0)
        inp=(c0>=o)&(c0<o+32)
        rank_update(W,XL,YR,inp)
        rank_update(V,XU,YT,inp)
        return 0
    lax.fori_loop(0,8,body,0)

def finish(U,LT,pk):
    r0=lax.broadcasted_iota(jnp.int32,(256,256),0); c0=lax.broadcasted_iota(jnp.int32,(256,256),1)
    eye=jnp.where(r0==c0,1.0,0.0).astype(BF)
    low=dotT(eye,LT[...].astype(BF))
    pk[...]=jnp.where(r0>c0,low,U[...]).astype(BF)


NR=16
NC=8
PC=16
MESH=pl.DeviceIdType.MESH

def front_kernel(mat, Lraw, Traw, pk0, pk1, li0, ut0, li1, ut1, l10, t01,
                 corner, W, V, U, LT, LI, UT,
                 c1s, c1r, c2s, c2r, c3s, c3r, d3s, d3r, tss, tsr, tgs, tgr, lss, lsr, lgs, lgr, loc):
    row=lax.axis_index("row"); col=lax.axis_index("col")
    cols=mat.shape[1]
    PL=mat.shape[0]//NC

    def rp_(j): return lax.rem(row+j,NR)
    def cp_(j): return lax.rem(col+j,NC)
    def rows(k,n=PC): return pl.ds(pl.multiple_of(k*n,n),n)
    def rc(src,dst,ss,rs,**dev):
        return pltpu.make_async_remote_copy(src_ref=src,dst_ref=dst,send_sem=ss,recv_sem=rs,device_id=dev,device_id_type=MESH)
    def loop(n,f):
        def b(j,_):
            f(j); return 0
        lax.fori_loop(1,n,b,0)

    bar=pltpu.get_barrier_semaphore()
    loop(NR,lambda j: pl.semaphore_signal(bar,inc=1,device_id={"row":rp_(j)},device_id_type=MESH))
    loop(NC,lambda j: pl.semaphore_signal(bar,inc=1,device_id={"col":cp_(j)},device_id_type=MESH))
    pl.semaphore_wait(bar,NR-1+NC-1)

    def own_corner(i,b,k): return mat.at[rows(k),0:NB], corner.at[b,rows(k)]
    def c1(i,jj,j):
        k=rp_(j); s,d=own_corner(i,2*i+jj,k)
        return rc(s,d,c1s.at[j],c1r.at[i],row=k)
    for i in range(2):
        for jj in range(2):
            @pl.when((row==i)&(col==jj))
            def _(i=i,jj=jj):
                s,d=own_corner(i,2*i+jj,row)
                pltpu.make_async_copy(s,d,loc.at[0]).start()
                loop(NR,lambda j: c1(i,jj,j).start())
                pltpu.make_async_copy(s,d,loc.at[0]).wait()
    def c2(i,jj,j):
        b=2*i+jj
        return rc(corner.at[b,rows(row)],corner.at[b,rows(row)],c2s.at[i,j],c2r.at[b],col=cp_(j))
    def c3(j):
        k=rp_(j); return rc(corner.at[0,rows(row)],corner.at[0,rows(row)],c3s.at[j],c3r.at[row],row=k)
    def d3(j):
        k=rp_(j); return rc(corner.at[1:4,rows(row)],corner.at[1:4,rows(row)],d3s.at[j],d3r.at[row],row=k)
    def c3w(j):
        k=rp_(j); rc(corner.at[0,rows(k)],corner.at[0,rows(k)],c3s.at[j],c3r.at[k],row=k).wait_recv()
    def d3w(j):
        k=rp_(j); rc(corner.at[1:4,rows(k)],corner.at[1:4,rows(k)],d3s.at[j],d3r.at[k],row=k).wait_recv()
    for i in range(2):
        for jj in range(2):
            @pl.when(col==jj)
            def _(i=i,jj=jj):
                @pl.when(row!=i)
                def _():
                    c1(i,jj,1).wait_recv()
                loop(NC,lambda j: c2(i,jj,j).start())
        if i==0:
            @pl.when(col!=0)
            def _(): c2(0,0,1).wait_recv()
            loop(NR,lambda j: c3(j).start())
    def ts(i,j):
        k=rp_(j); return rc(mat.at[rows(k)],Traw.at[i,rows(k)],tss.at[j],tsr.at[i],row=k)
    def ls(i,j):
        k=cp_(j); return rc(mat.at[rows(k,PL),0:NB],Lraw.at[i,rows(k,PL)],lss.at[j],lsr.at[i],col=k)
    def tl(i): return pltpu.make_async_copy(mat.at[rows(row)],Traw.at[i,rows(row)],loc.at[1])
    def ll(i): return pltpu.make_async_copy(mat.at[rows(col,PL),0:NB],Lraw.at[i,rows(col,PL)],loc.at[2])
    for i in range(2):
        @pl.when(row==i)
        def _(i=i):
            tl(i).start(); loop(NR,lambda j: ts(i,j).start())
        @pl.when(col==i)
        def _(i=i):
            ll(i).start(); loop(NC,lambda j: ls(i,j).start())
    for b in (1,2,3):
        @pl.when(col!=b%2)
        def _(b=b): c2(b//2,b%2,1).wait_recv()
    loop(NR,lambda j: d3(j).start())
    loop(NR,c3w)

    def tg(i,j):
        k=rp_(j); return rc(Traw.at[i,rows(row)],Traw.at[i,rows(row)],tgs.at[i,j],tgr.at[i,row],row=k)
    def lg(i,j):
        k=cp_(j); return rc(Lraw.at[i,rows(col,PL)],Lraw.at[i,rows(col,PL)],lgs.at[i,j],lgr.at[i,col],col=k)
    def tgw(i,j):
        k=rp_(j); rc(Traw.at[i,rows(k)],Traw.at[i,rows(k)],tgs.at[i,j],tgr.at[i,k],row=k).wait_recv()
    def lgw(i,j):
        k=cp_(j); rc(Lraw.at[i,rows(k,PL)],Lraw.at[i,rows(k,PL)],lgs.at[i,j],lgr.at[i,k],col=k).wait_recv()
    def gather(i):
        @pl.when(col==i)
        def _(): ll(i).wait()
        @pl.when(col!=i)
        def _(): ls(i,1).wait_recv()
        loop(NC,lambda j: lg(i,j).start())
        @pl.when(row==i)
        def _(): tl(i).wait()
        @pl.when(row!=i)
        def _(): ts(i,1).wait_recv()
        loop(NR,lambda j: tg(i,j).start())

    def dump(li,ut):
        for ref,src in ((li,LI),(ut,UT)):
            for n,x in enumerate(split2(src[...])): ref[n]=x
    lu_inv(corner[0],W,V,U,LT,LI,UT,((HOOK0,lambda: gather(0)),(HOOK1,lambda: gather(1))))
    finish(U,LT,pk0); dump(li0,ut0)
    loop(NR,d3w)
    L=sum(dotT(corner[2],ut0[n]) for n in (1,0)).astype(BF)
    T=sum(jnp.dot(li0[n],corner[1],preferred_element_type=F) for n in (1,0)).astype(BF)
    l10[...]=L; t01[...]=T
    a=(corner[3].astype(F)-jnp.dot(L,T,preferred_element_type=F)).astype(BF)
    lu_inv(a,W,V,U,LT,LI,UT)
    finish(U,LT,pk1); dump(li1,ut1)
    for i in range(2):
        loop(NC,lambda j: lgw(i,j))
        loop(NR,lambda j: tgw(i,j))
    for i in range(2):
        for jj in range(2):
            @pl.when((row==i)&(col==jj))
            def _(i=i,jj=jj): loop(NR,lambda j: c1(i,jj,j).wait_send())
            @pl.when(col==jj)
            def _(i=i,jj=jj): loop(NC,lambda j: c2(i,jj,j).wait_send())
        @pl.when(row==i)
        def _(i=i): loop(NR,lambda j: ts(i,j).wait_send())
        @pl.when(col==i)
        def _(i=i): loop(NC,lambda j: ls(i,j).wait_send())
        loop(NC,lambda j: lg(i,j).wait_send())
        loop(NR,lambda j: tg(i,j).wait_send())
    loop(NR,lambda j: c3(j).wait_send())
    loop(NR,lambda j: d3(j).wait_send())

HOOK0=3
HOOK1=5

def front(mat):
    rows_,cols_=mat.shape
    vm=pl.BlockSpec(memory_space=pltpu.VMEM); an=pl.BlockSpec(memory_space=pl.ANY)
    s=jax.ShapeDtypeStruct((NB,NB),BF); s2=jax.ShapeDtypeStruct((2,NB,NB),BF)
    dma=pltpu.SemaphoreType.DMA
    return pl.pallas_call(front_kernel,
        out_shape=[jax.ShapeDtypeStruct((2,rows_,NB),BF),jax.ShapeDtypeStruct((2,NB,cols_),BF),s,s,s2,s2,s2,s2,s,s],
        in_specs=[an],out_specs=[an,an]+[vm]*8,
        scratch_shapes=[pltpu.VMEM((4,NB,NB),BF)]+[pltpu.VMEM((NB,NB),F)]*6+[
            dma((NR,)),dma((2,)),dma((2,NC)),dma((4,)),dma((NR,)),dma((NR,)),dma((NR,)),dma((NR,)),
            dma((NR,)),dma((2,)),dma((2,NR)),dma((2,NR)),dma((NC,)),dma((2,)),dma((2,NC)),dma((2,NC)),dma((3,))],
        compiler_params=pltpu.CompilerParams(collective_id=0,has_side_effects=True,vmem_limit_bytes=40*2**20))(mat)

def update_kernel(a, lraw, traw, pk0, pk1, li0, ut0, li1, ut1, l10, t01, out, T0, T1):
    t=pl.program_id(0)
    row=lax.axis_index("row"); col=lax.axis_index("col")
    cols=a.shape[1]
    CH=cols//7
    def mm(x,y): return jnp.dot(x,y,preferred_element_type=F)
    @pl.when(t==0)
    def _():
        for c in range(7):
            w=pl.ds(c*CH,CH)
            x=traw[0,:,w]
            y=(mm(li0[1],x)+mm(li0[0],x)).astype(BF)
            T0[:,w]=y
            z=(traw[1,:,w].astype(F)-mm(l10[...],y)).astype(BF)
            T1[:,w]=(mm(li1[1],z)+mm(li1[0],z)).astype(BF)
    x=lraw[0]
    L0=(dotT(x,ut0[1])+dotT(x,ut0[0])).astype(BF)
    z=(lraw[1].astype(F)-mm(L0,t01[...])).astype(BF)
    L1=(dotT(z,ut1[1])+dotT(z,ut1[0])).astype(BF)
    for c in range(7):
        w=pl.ds(c*CH,CH)
        y=(a[:,w].astype(F)-mm(L0,T0[:,w])).astype(BF)
        out[:,w]=(y.astype(F)-mm(L1,T1[:,w])).astype(BF)
    @pl.when(col==0)
    def _(): out[:,0:NB]=L0
    @pl.when(col==1)
    def _(): out[:,0:NB]=L1
    @pl.when((t==0)&(row==0))
    def _():
        out[...]=T0[...]
        @pl.when(col==0)
        def _(): out[:,0:NB]=pk0[...]
    @pl.when((t==0)&(row==1))
    def _():
        out[:,NB:]=T1[:,NB:]
        @pl.when(col==1)
        def _(): out[:,0:NB]=pk1[...]
        @pl.when(col>1)
        def _(): out[:,0:NB]=T1[:,0:NB]

def update(mat, Lraw, Traw, *small):
    rows_,cols_=mat.shape
    vm=pl.BlockSpec(memory_space=pltpu.VMEM)
    return pl.pallas_call(update_kernel,grid=(rows_//NB,),
        out_shape=jax.ShapeDtypeStruct(mat.shape,BF),
        in_specs=[pl.BlockSpec((NB,cols_),lambda t:(t,0)),pl.BlockSpec((2,NB,NB),lambda t:(0,t,0)),vm]+[vm]*8,
        out_specs=pl.BlockSpec((NB,cols_),lambda t:(t,0)),
        scratch_shapes=[pltpu.VMEM((NB,cols_),BF)]*2,
        compiler_params=pltpu.CompilerParams(vmem_limit_bytes=50*2**20))(mat,Lraw,Traw,*small)

def on_device(mat):
    return update(mat,*front(mat))

def solution(mesh):
    return jax.shard_map(on_device,mesh=mesh,in_specs=(P("row","col"),),out_specs=P("row","col"),check_vma=False)
```

```python
import functools
import jax, jax.numpy as jnp
from jax import lax
from jax.experimental import pallas as pl
from jax.experimental.pallas import tpu as pltpu
from jax.sharding import PartitionSpec as P
NB=256
F=jnp.float32
BF=jnp.bfloat16

def split2(x):
    hi=x.astype(BF); lo=(x-hi.astype(F)).astype(BF)
    return hi,lo
def dotT(a,b):
    return lax.dot_general(a,b,(((1,),(1,)),((),())),preferred_element_type=F)

def sub_bcast(x,i):
    return jnp.broadcast_to(x[i:i+1,:],(8,128))

def recip(p):
    r=pl.reciprocal(p,approx=True)
    r=r*(2.0-p*r)
    r=r*(2.0-p*r)
    return r

def panel(q, PR, PT, sub, lane):
    base=(q%4)*32
    hi=(q>=4)
    E=[jnp.where(lane==base+8*g+sub,1.0,0.0).astype(F) for g in range(4)]
    E2=list(E)
    rpv=[jnp.zeros((8,128),F) for _ in range(4)]
    for s in range(4):
        idx=[jnp.full((8,128),base+8*s+m,jnp.int32) for m in range(8)]
        R=[[None]*4 for _ in range(8)]; Q=[[None]*4 for _ in range(8)]
        for g in range(s,4):
            tr=jnp.where(hi,PR[g][1],PR[g][0]); tt=jnp.where(hi,PT[g][1],PT[g][0])
            for m in range(8):
                R[m][g]=jnp.take_along_axis(tr,idx[m],axis=1,mode="promise_in_bounds")
                Q[m][g]=jnp.take_along_axis(tt,idx[m],axis=1,mode="promise_in_bounds")
        for i in range(8):
            rp=recip(sub_bcast(R[i][s],i))
            rpv[s]=jnp.where(sub==i,rp,rpv[s])
            pr=[sub_bcast(PR[s][h],i) for h in range(2)]+[sub_bcast(E[s],i)]
            pt=[sub_bcast(PT[s][h],i) for h in range(2)]+[sub_bcast(E2[s],i)]
            rb={m:sub_bcast(R[m][s],i) for m in range(i+1,8)}
            qb={m:sub_bcast(Q[m][s],i) for m in range(i+1,8)}
            for g in range(s,4):
                l=R[i][g]*rp; u=Q[i][g]*rp
                if g==s:
                    if i==7: continue
                    l=jnp.where(sub>i,l,0.0); u=jnp.where(sub>i,u,0.0)
                for m in range(i+1,8):
                    R[m][g]=R[m][g]-l*rb[m]
                    Q[m][g]=Q[m][g]-u*qb[m]
                for h in range(2):
                    PR[g][h]=PR[g][h]-l*pr[h]
                    PT[g][h]=PT[g][h]-u*pt[h]
                E[g]=E[g]-l*pr[2]
                E2[g]=E2[g]-u*pt[2]
    return PR,PT,E,E2,rpv

def rank_update(ref, XT, Y, inp):
    xh,xl=split2(XT); yh,yl=split2(Y)
    X=jnp.concatenate([xh,xh,xl],axis=0)
    Y3=jnp.concatenate([yh,yl,yh],axis=0)
    up=lax.dot_general(X,Y3,(((0,),(0,)),((),())),preferred_element_type=F)
    ref[...]=jnp.where(inp,0.0,ref[...])-up

def lu_inv(a_bf, W, V, U, LT, LI, UT, hooks=()):
    r0=lax.broadcasted_iota(jnp.int32,(256,256),0); c0=lax.broadcasted_iota(jnp.int32,(256,256),1)
    eye=jnp.where(r0==c0,1.0,0.0).astype(BF)
    W[...]=a_bf.astype(F)
    V[...]=dotT(eye,a_bf)
    sub=lax.broadcasted_iota(jnp.int32,(8,128),0); lane=lax.broadcasted_iota(jnp.int32,(8,128),1)
    def body(q,_):
        for at, hook in hooks:
            pl.when(q==at)(hook)
        o=pl.multiple_of(q*32,32)
        PR=[[W[pl.ds(o+8*g,8),128*h:128*h+128] for h in range(2)] for g in range(4)]
        PT=[[V[pl.ds(o+8*g,8),128*h:128*h+128] for h in range(2)] for g in range(4)]
        PR,PT,E,E2,rpv=panel(q,PR,PT,sub,lane)
        XL=[];XU=[];YR=[];YT=[]
        for g in range(4):
            a=[];b=[];c=[];d=[]
            for h in range(2):
                gl=lane+128*h
                inp=(gl>=o)&(gl<o+32); right=gl>=o+32; left=gl<o
                ur=PR[g][h]; ut=PT[g][h]
                lt=ut*rpv[g]; un=ur*rpv[g]
                U[pl.ds(o+8*g,8),128*h:128*h+128]=ur
                LT[pl.ds(o+8*g,8),128*h:128*h+128]=lt
                mr=jnp.where(inp,E[g],ur); mt=jnp.where(inp,E2[g],ut)
                LI[pl.ds(o+8*g,8),128*h:128*h+128]=jnp.where(right,0.0,mr)
                UT[pl.ds(o+8*g,8),128*h:128*h+128]=jnp.where(right,0.0,mt*rpv[g])
                a.append(jnp.where(right,lt,0.0)); b.append(jnp.where(right,un,0.0)); c.append(mr); d.append(mt)
            XL.append(jnp.concatenate(a,1)); XU.append(jnp.concatenate(b,1)); YR.append(jnp.concatenate(c,1)); YT.append(jnp.concatenate(d,1))
        XL=jnp.concatenate(XL,0);XU=jnp.concatenate(XU,0);YR=jnp.concatenate(YR,0);YT=jnp.concatenate(YT,0)
        inp=(c0>=o)&(c0<o+32)
        rank_update(W,XL,YR,inp)
        rank_update(V,XU,YT,inp)
        return 0
    lax.fori_loop(0,8,body,0)

def finish(U,LT,pk):
    r0=lax.broadcasted_iota(jnp.int32,(256,256),0); c0=lax.broadcasted_iota(jnp.int32,(256,256),1)
    eye=jnp.where(r0==c0,1.0,0.0).astype(BF)
    low=dotT(eye,LT[...].astype(BF))
    pk[...]=jnp.where(r0>c0,low,U[...]).astype(BF)


NR=16
NC=8
NY=4
CP=NB//NC
MESH=pl.DeviceIdType.MESH
AT=dict(d3=(1,),lg=(2,),s2=(3,1),g1=(6,4),g2=(8,6))

def front_kernel(mat, Lout, Tout, pk0, pk1,
                 Lraw, Traw, li0, ut0, li1, ut1, l10, t01, corner, W, V, U, LT, LI, UT,
                 p1s, p1r, p2s, p2r, c3s, c3r, d3s, d3r, lss, lsr, lgs, lgr,
                 s1s, s1r, s2s, s2p, s2r, g1s, g1r, g2s, g2r, loc):
    row=lax.axis_index("row"); col=lax.axis_index("col")
    y=lax.rem(row,NY); z=row//NY
    cols=mat.shape[1]
    PL=mat.shape[0]//NC
    H=cols//2

    def rp_(j): return lax.rem(row+j,NR)
    def cp_(j): return lax.rem(col+j,NC)
    def rows(k,n): return pl.ds(pl.multiple_of(k*n,n),n)
    def rc(src,dst,ss,rs,**dev):
        return pltpu.make_async_remote_copy(src_ref=src,dst_ref=dst,send_sem=ss,recv_sem=rs,device_id=dev,device_id_type=MESH)
    def loop(n,f):
        def b(j,_):
            f(j); return 0
        lax.fori_loop(1,n,b,0)

    bar=pltpu.get_barrier_semaphore()
    loop(NR,lambda j: pl.semaphore_signal(bar,inc=1,device_id={"row":rp_(j)},device_id_type=MESH))
    loop(NC,lambda j: pl.semaphore_signal(bar,inc=1,device_id={"col":cp_(j)},device_id_type=MESH))
    pl.semaphore_wait(bar,NR-1+NC-1)

    Q=NB//NY; PC=Q//NY
    def nx(v,d): return lax.rem(v+d,NY)
    def half(h): return slice(0,H) if h==0 else slice(H,2*H)
    def ab(h): return (z,y) if h==0 else (y,z)
    def dev(h,a,b): return a*NY+b if h==0 else b*NY+a
    def qref(ref,h,a): return ref.at[rows(a,Q),half(h)]
    def tq(i,h,a): return Traw.at[i,rows(a,Q),half(h)]
    def s1(i,h,d):
        a,b=ab(h); a2=nx(a,d)
        return rc(qref(mat,h,a2),tq(i,h,a2),s1s.at[h,d],s1r.at[i,h],row=dev(h,a2,b))
    def s1l(i,h):
        a,b=ab(h); return pltpu.make_async_copy(qref(mat,h,a),tq(i,h,a),loc.at[1+h])
    def scatter(i):
        @pl.when(row==i)
        def _():
            for h in range(2):
                s1l(i,h).start(); loop(NY,lambda d: s1(i,h,d).start())
    def p1(b,j):
        c=cp_(j); return rc(mat.at[rows(c,CP),0:NB],corner.at[b,rows(c,CP)],p1s.at[j],p1r.at[b%2],col=c)
    def p1w(b):
        pl.when(col!=b%2)(lambda: p1(b,1).wait_recv())
    for i in range(2):
        for jj in range(2):
            @pl.when((row==i)&(col==jj))
            def _(b=2*i+jj):
                cc=pltpu.make_async_copy(mat.at[rows(col,CP),0:NB],corner.at[b,rows(col,CP)],loc.at[0])
                cc.start()
                loop(NC,lambda j: p1(b,j).start())
                cc.wait()
    scatter(1)
    mine=rows(col,CP)
    def p2(n,j):
        r=(corner.at[0,mine],corner.at[1,mine],corner.at[2:4,mine])[n]
        return rc(r,r,p2s.at[n,j],p2r.at[n],row=rp_(j))
    def c3(j): return rc(corner.at[0,mine],corner.at[0,mine],c3s.at[j],c3r.at[col],col=cp_(j))
    def d3(j): return rc(corner.at[1:4,mine],corner.at[1:4,mine],d3s.at[j],d3r.at[col],col=cp_(j))
    def c3w(j):
        c=cp_(j); rc(corner.at[0,rows(c,CP)],corner.at[0,rows(c,CP)],c3s.at[j],c3r.at[c],col=c).wait_recv()
    def d3w(j):
        c=cp_(j); rc(corner.at[1:4,rows(c,CP)],corner.at[1:4,rows(c,CP)],d3s.at[j],d3r.at[c],col=c).wait_recv()
    @pl.when(row==0)
    def _():
        p1w(0); loop(NR,lambda j: p2(0,j).start())
    @pl.when(row!=0)
    def _(): p2(0,1).wait_recv()
    loop(NC,lambda j: c3(j).start())

    def ls(i,j):
        k=cp_(j); return rc(mat.at[rows(k,PL),0:NB],Lraw.at[i,rows(k,PL)],lss.at[j],lsr.at[i],col=k)
    def ll(i): return pltpu.make_async_copy(mat.at[rows(col,PL),0:NB],Lraw.at[i,rows(col,PL)],loc.at[3])
    def lg(i,j):
        k=cp_(j); return rc(Lraw.at[i,rows(col,PL)],Lraw.at[i,rows(col,PL)],lgs.at[i,j],lgr.at[i,col],col=k)
    def lgw(i,j):
        k=cp_(j); rc(Lraw.at[i,rows(k,PL)],Lraw.at[i,rows(k,PL)],lgs.at[i,j],lgr.at[i,k],col=k).wait_recv()
    def left_gather():
        for i in range(2):
            pl.when(col==i)(lambda: ll(i).wait())
            pl.when(col!=i)(lambda: ls(i,1).wait_recv())
            loop(NC,lambda j: lg(i,j).start())

    def src_ab(h,i): return (0,i) if h==0 else (i,0)
    def tp(i,h,a,b): return Traw.at[i,rows(a*NY+b,PC),half(h)]
    def s2(i,h,d):
        a,b=ab(h); b2=nx(b,d)
        return rc(tp(i,h,a,b2),tp(i,h,a,b2),s2s.at[i,h,d],s2r.at[i,h],row=dev(h,a,b2))
    def g1(i,h,d,ss):
        a,b=ab(h); b2=nx(b,d)
        return rc(tp(i,h,a,b),tp(i,h,a,b),ss.at[i,h,d],g1r.at[i,h,b],row=dev(h,a,b2))
    def g1w(i,h,d):
        a,b=ab(h); b2=nx(b,d)
        rc(tp(i,h,a,b2),tp(i,h,a,b2),g1s.at[i,h,d],g1r.at[i,h,b2],row=dev(h,a,b2)).wait_recv()
    def g2(i,h,d):
        a,b=ab(h); a2=nx(a,d)
        return rc(tq(i,h,a),tq(i,h,a),g2s.at[i,h,d],g2r.at[i,h,a],row=dev(h,a2,b))
    def g2w(i,h,d):
        a,b=ab(h); a2=nx(a,d)
        rc(tq(i,h,a2),tq(i,h,a2),g2s.at[i,h,d],g2r.at[i,h,a2],row=dev(h,a2,b)).wait_recv()
    each=[(i,h) for i in range(2) for h in range(2)]
    def inner_is_src(i,h): return ab(h)[1]==src_ab(h,i)[1]
    def top_s2(n):
        for i,h in each:
            if i!=n: continue
            @pl.when(inner_is_src(i,h))
            def _(i=i,h=h):
                pl.when(row==i)(lambda: s1l(i,h).wait())
                pl.when(row!=i)(lambda: s1(i,h,1).wait_recv())
                def f(d):
                    s2(i,h,d).start(); g1(i,h,d,s2p).start()
                loop(NY,f)
    def top_g1(n):
        for i,h in each:
            if i!=n: continue
            sb=src_ab(h,i)[1]; b=ab(h)[1]
            @pl.when(b!=sb)
            def _(i=i,h=h,sb=sb,b=b):
                s2(i,h,1).wait_recv()
                loop(NY,lambda d: pl.when(nx(b,d)!=sb)(lambda: g1(i,h,d,g1s).start()))
    def top_g2(n):
        for i,h in each:
            if i!=n: continue
            @pl.when(ab(h)[1]!=src_ab(h,i)[1])
            def _(i=i,h=h): loop(NY,lambda d: g1w(i,h,d))
            loop(NY,lambda d: g2(i,h,d).start())

    for i in range(2):
        if i==0: scatter(0)
        @pl.when(col==i)
        def _(i=i):
            ll(i).start(); loop(NC,lambda j: ls(i,j).start())
    @pl.when(row==0)
    def _():
        p1w(1); loop(NR,lambda j: p2(1,j).start())
    @pl.when(row==1)
    def _():
        p1w(2); p1w(3); loop(NR,lambda j: p2(2,j).start())
    loop(NC,c3w)
    def rest_corners():
        pl.when(row!=0)(lambda: p2(1,1).wait_recv())
        pl.when(row!=1)(lambda: p2(2,1).wait_recv())
        loop(NC,lambda j: d3(j).start())

    def dump(li,ut):
        for ref,src in ((li,LI),(ut,UT)):
            for n,x in enumerate(split2(src[...])): ref[n]=x
    acts=[(AT["d3"][0],rest_corners),(AT["lg"][0],left_gather)]
    for f,n in ((top_s2,"s2"),(top_g1,"g1"),(top_g2,"g2")):
        acts+=[(AT[n][k],functools.partial(f,k)) for k in (0,1)]
    lu_inv(corner[0],W,V,U,LT,LI,UT,[x for x in acts if x[0]<8])
    finish(U,LT,pk0); dump(li0,ut0)
    loop(NC,d3w)
    L=sum(dotT(corner[2],ut0[n]) for n in (1,0)).astype(BF)
    T=sum(jnp.dot(li0[n],corner[1],preferred_element_type=F) for n in (1,0)).astype(BF)
    l10[...]=L; t01[...]=T
    a=(corner[3].astype(F)-jnp.dot(L,T,preferred_element_type=F)).astype(BF)
    lu_inv(a,W,V,U,LT,LI,UT,[(x[0]-8,x[1]) for x in acts if x[0]>=8])
    finish(U,LT,pk1); dump(li1,ut1)
    for i in range(2):
        loop(NC,lambda j: lgw(i,j))
    def mm(x,y): return jnp.dot(x,y,preferred_element_type=F)
    LB=NB
    def lsolve(k,_):
        w=pl.ds(pl.multiple_of(k*LB,LB),LB)
        x=Lraw[0,w]
        x=(dotT(x,ut0[1])+dotT(x,ut0[0])).astype(BF)
        Lout[0,w]=x
        x=(Lraw[1,w].astype(F)-mm(x,t01[...])).astype(BF)
        Lout[1,w]=(dotT(x,ut1[1])+dotT(x,ut1[0])).astype(BF)
        return 0
    lax.fori_loop(0,mat.shape[0]//LB,lsolve,0)
    TB=cols//7
    for i,h in each:
        if i==0: loop(NY,lambda d: g2w(i,h,d))
    def tsolve0(k,_):
        w=pl.ds(pl.multiple_of(k*TB,TB),TB)
        x=Traw[0,:,w]
        Tout[0,:,w]=(mm(li0[1],x)+mm(li0[0],x)).astype(BF)
        return 0
    lax.fori_loop(0,7,tsolve0,0)
    for i,h in each:
        if i==1: loop(NY,lambda d: g2w(i,h,d))
    def tsolve1(k,_):
        w=pl.ds(pl.multiple_of(k*TB,TB),TB)
        x=(Traw[1,:,w].astype(F)-mm(l10[...],Tout[0,:,w])).astype(BF)
        Tout[1,:,w]=(mm(li1[1],x)+mm(li1[0],x)).astype(BF)
        return 0
    lax.fori_loop(0,7,tsolve1,0)
    for i in range(2):
        for jj in range(2):
            pl.when((row==i)&(col==jj))(lambda: loop(NC,lambda j: p1(2*i+jj,j).wait_send()))
        pl.when(col==i)(lambda: loop(NC,lambda j: ls(i,j).wait_send()))
        loop(NC,lambda j: lg(i,j).wait_send())
    pl.when(row==0)(lambda: loop(NR,lambda j: (p2(0,j).wait_send(),p2(1,j).wait_send())))
    pl.when(row==1)(lambda: loop(NR,lambda j: p2(2,j).wait_send()))
    loop(NC,lambda j: (c3(j).wait_send(),d3(j).wait_send()))
    for i,h in each:
        b=ab(h)[1]; sb=src_ab(h,i)[1]
        pl.when(row==i)(lambda: loop(NY,lambda d: s1(i,h,d).wait_send()))
        pl.when(b==sb)(lambda: loop(NY,lambda d: (s2(i,h,d).wait_send(),g1(i,h,d,s2p).wait_send())))
        pl.when(b!=sb)(lambda: loop(NY,lambda d: pl.when(nx(b,d)!=sb)(lambda: g1(i,h,d,g1s).wait_send())))
        loop(NY,lambda d: g2(i,h,d).wait_send())

def front(mat):
    rows_,cols_=mat.shape
    vm=pl.BlockSpec(memory_space=pltpu.VMEM); an=pl.BlockSpec(memory_space=pl.ANY)
    s=jax.ShapeDtypeStruct((NB,NB),BF)
    dma=pltpu.SemaphoreType.DMA
    return pl.pallas_call(front_kernel,
        out_shape=[jax.ShapeDtypeStruct((2,rows_,NB),BF),jax.ShapeDtypeStruct((2,NB,cols_),BF),s,s],
        in_specs=[an],out_specs=[vm]*4,
        scratch_shapes=[pltpu.VMEM((2,rows_,NB),BF),pltpu.VMEM((2,NB,cols_),BF)]+[pltpu.VMEM((2,NB,NB),BF)]*4+[pltpu.VMEM((NB,NB),BF)]*2+[pltpu.VMEM((4,NB,NB),BF)]+[pltpu.VMEM((NB,NB),F)]*6+[
            dma((NC,)),dma((2,)),dma((3,NR)),dma((3,)),dma((NC,)),dma((NC,)),dma((NC,)),dma((NC,)),
            dma((NC,)),dma((2,)),dma((2,NC)),dma((2,NC)),
            dma((2,NY)),dma((2,2)),dma((2,2,NY)),dma((2,2,NY)),dma((2,2)),dma((2,2,NY)),dma((2,2,NY)),dma((2,2,NY)),dma((2,2,NY)),dma((4,))],
        compiler_params=pltpu.CompilerParams(collective_id=0,has_side_effects=True,vmem_limit_bytes=40*2**20))(mat)

def update_kernel(a, L, T, pk0, pk1, out):
    t=pl.program_id(0)
    row=lax.axis_index("row"); col=lax.axis_index("col")
    def mm(x,y): return jnp.dot(x,y,preferred_element_type=F)
    for r in range(a.shape[0]//NB):
        w=pl.ds(r*NB,NB)
        y=(a[w].astype(F)-mm(L[0,w],T[0])).astype(BF)
        out[w]=(y.astype(F)-mm(L[1,w],T[1])).astype(BF)
    for c in range(2):
        @pl.when((t==0)&(col==c))
        def _(c=c): out[:,0:NB]=L[c]
    @pl.when(row==0)
    def _():
        out[0:NB]=T[0]
        @pl.when((t==0)&(col==0))
        def _(): out[0:NB,0:NB]=pk0[...]
    @pl.when(row==1)
    def _():
        out[0:NB,NB:]=T[1,:,NB:]
        @pl.when((t>0)|(col>1))
        def _(): out[0:NB,0:NB]=T[1,:,0:NB]
        @pl.when((t==0)&(col==1))
        def _(): out[0:NB,0:NB]=pk1[...]

CW=512

def update(mat, L, T, pk0, pk1):
    rows_,cols_=mat.shape
    vm=pl.BlockSpec(memory_space=pltpu.VMEM)
    return pl.pallas_call(update_kernel,grid=(cols_//CW,),
        out_shape=jax.ShapeDtypeStruct(mat.shape,BF),
        in_specs=[pl.BlockSpec((rows_,CW),lambda t:(0,t)),vm,pl.BlockSpec((2,NB,CW),lambda t:(0,0,t)),vm,vm],
        out_specs=pl.BlockSpec((rows_,CW),lambda t:(0,t)),
        compiler_params=pltpu.CompilerParams(vmem_limit_bytes=40*2**20))(mat,L,T,pk0,pk1)

def on_device(mat):
    return update(mat,*front(mat))

def solution(mesh):
    return jax.shard_map(on_device,mesh=mesh,in_specs=(P("row","col"),),out_specs=P("row","col"),check_vma=False)
```

```python
import functools
import jax, jax.numpy as jnp
from jax import lax
from jax.experimental import pallas as pl
from jax.experimental.pallas import tpu as pltpu
from jax.sharding import PartitionSpec as P
NB=256
F=jnp.float32
BF=jnp.bfloat16

def split2(x):
    hi=x.astype(BF); lo=(x-hi.astype(F)).astype(BF)
    return hi,lo
def dotT(a,b):
    return lax.dot_general(a,b,(((1,),(1,)),((),())),preferred_element_type=F)

def sub_bcast(x,i):
    return jnp.broadcast_to(x[i:i+1,:],(8,128))

def recip(p):
    r=pl.reciprocal(p,approx=True)
    r=r*(2.0-p*r)
    r=r*(2.0-p*r)
    return r

def panel(q, PR, PT, sub, lane):
    base=(q%4)*32
    hi=(q>=4)
    E=[jnp.where(lane==base+8*g+sub,1.0,0.0).astype(F) for g in range(4)]
    E2=list(E)
    rpv=[jnp.zeros((8,128),F) for _ in range(4)]
    for s in range(4):
        idx=[jnp.full((8,128),base+8*s+m,jnp.int32) for m in range(8)]
        R=[[None]*4 for _ in range(8)]; Q=[[None]*4 for _ in range(8)]
        for g in range(s,4):
            tr=jnp.where(hi,PR[g][1],PR[g][0]); tt=jnp.where(hi,PT[g][1],PT[g][0])
            for m in range(8):
                R[m][g]=jnp.take_along_axis(tr,idx[m],axis=1,mode="promise_in_bounds")
                Q[m][g]=jnp.take_along_axis(tt,idx[m],axis=1,mode="promise_in_bounds")
        for i in range(8):
            rp=recip(sub_bcast(R[i][s],i))
            rpv[s]=jnp.where(sub==i,rp,rpv[s])
            pr=[sub_bcast(PR[s][h],i) for h in range(2)]+[sub_bcast(E[s],i)]
            pt=[sub_bcast(PT[s][h],i) for h in range(2)]+[sub_bcast(E2[s],i)]
            rb={m:sub_bcast(R[m][s],i) for m in range(i+1,8)}
            qb={m:sub_bcast(Q[m][s],i) for m in range(i+1,8)}
            for g in range(s,4):
                l=R[i][g]*rp; u=Q[i][g]*rp
                if g==s:
                    if i==7: continue
                    l=jnp.where(sub>i,l,0.0); u=jnp.where(sub>i,u,0.0)
                for m in range(i+1,8):
                    R[m][g]=R[m][g]-l*rb[m]
                    Q[m][g]=Q[m][g]-u*qb[m]
                for h in range(2):
                    PR[g][h]=PR[g][h]-l*pr[h]
                    PT[g][h]=PT[g][h]-u*pt[h]
                E[g]=E[g]-l*pr[2]
                E2[g]=E2[g]-u*pt[2]
    return PR,PT,E,E2,rpv

def rank_update(ref, XT, Y, inp):
    xh,xl=split2(XT); yh,yl=split2(Y)
    X=jnp.concatenate([xh,xh,xl],axis=0)
    Y3=jnp.concatenate([yh,yl,yh],axis=0)
    up=lax.dot_general(X,Y3,(((0,),(0,)),((),())),preferred_element_type=F)
    ref[...]=jnp.where(inp,0.0,ref[...])-up

def lu_inv(a_bf, W, V, U, LT, LI, UT, hooks=()):
    r0=lax.broadcasted_iota(jnp.int32,(256,256),0); c0=lax.broadcasted_iota(jnp.int32,(256,256),1)
    eye=jnp.where(r0==c0,1.0,0.0).astype(BF)
    W[...]=a_bf.astype(F)
    V[...]=dotT(eye,a_bf)
    sub=lax.broadcasted_iota(jnp.int32,(8,128),0); lane=lax.broadcasted_iota(jnp.int32,(8,128),1)
    def body(q,_):
        for at, hook in hooks:
            pl.when(q==at)(hook)
        o=pl.multiple_of(q*32,32)
        PR=[[W[pl.ds(o+8*g,8),128*h:128*h+128] for h in range(2)] for g in range(4)]
        PT=[[V[pl.ds(o+8*g,8),128*h:128*h+128] for h in range(2)] for g in range(4)]
        PR,PT,E,E2,rpv=panel(q,PR,PT,sub,lane)
        XL=[];XU=[];YR=[];YT=[]
        for g in range(4):
            a=[];b=[];c=[];d=[]
            for h in range(2):
                gl=lane+128*h
                inp=(gl>=o)&(gl<o+32); right=gl>=o+32; left=gl<o
                ur=PR[g][h]; ut=PT[g][h]
                lt=ut*rpv[g]; un=ur*rpv[g]
                U[pl.ds(o+8*g,8),128*h:128*h+128]=ur
                LT[pl.ds(o+8*g,8),128*h:128*h+128]=lt
                mr=jnp.where(inp,E[g],ur); mt=jnp.where(inp,E2[g],ut)
                LI[pl.ds(o+8*g,8),128*h:128*h+128]=jnp.where(right,0.0,mr)
                UT[pl.ds(o+8*g,8),128*h:128*h+128]=jnp.where(right,0.0,mt*rpv[g])
                a.append(jnp.where(right,lt,0.0)); b.append(jnp.where(right,un,0.0)); c.append(mr); d.append(mt)
            XL.append(jnp.concatenate(a,1)); XU.append(jnp.concatenate(b,1)); YR.append(jnp.concatenate(c,1)); YT.append(jnp.concatenate(d,1))
        XL=jnp.concatenate(XL,0);XU=jnp.concatenate(XU,0);YR=jnp.concatenate(YR,0);YT=jnp.concatenate(YT,0)
        inp=(c0>=o)&(c0<o+32)
        rank_update(W,XL,YR,inp)
        rank_update(V,XU,YT,inp)
        return 0
    lax.fori_loop(0,8,body,0)

def finish(U,LT,pk):
    r0=lax.broadcasted_iota(jnp.int32,(256,256),0); c0=lax.broadcasted_iota(jnp.int32,(256,256),1)
    eye=jnp.where(r0==c0,1.0,0.0).astype(BF)
    low=dotT(eye,LT[...].astype(BF))
    pk[...]=jnp.where(r0>c0,low,U[...]).astype(BF)


NR=16
NC=8
NY=4
CP=NB//NC
MESH=pl.DeviceIdType.MESH
AT=dict(d3=(1,),lg=(4,),s2=(3,1),g1=(6,4),g2=(8,6),g3=(13,11))

def front_kernel(mat, Lout, Tout, pk0, pk1,
                 Lraw, Traw, li0, ut0, li1, ut1, l10, t01, corner, W, V, U, LT, LI, UT,
                 p1s, p1r, p2s, p2r, c3s, c3r, d3s, d3r, lss, lsr, lgs, lgr,
                 s1s, s1r, s2s, s2p, s2r, g1s, g1r, g2s, g2r, g3s, g3r, loc):
    row=lax.axis_index("row"); col=lax.axis_index("col")
    y=jnp.bitwise_and(row,NY-1); z=jnp.right_shift(row,2)
    cols=mat.shape[1]
    PL=mat.shape[0]//NC
    H=cols//2

    def rp_(j): return jnp.bitwise_and(row+j,NR-1)
    def cp_(j): return jnp.bitwise_and(col+j,NC-1)
    def rows(k,n): return pl.ds(pl.multiple_of(k*n,n),n)
    def rc(src,dst,ss,rs,**dev):
        to=(dev.get("row",row),dev.get("col",col))
        return pltpu.make_async_remote_copy(src_ref=src,dst_ref=dst,send_sem=ss,recv_sem=rs,device_id=to,device_id_type=MESH)
    def took(ref,sem): pltpu.make_async_copy(ref,ref,sem).wait()
    def loop(n,f):
        for j in range(1,n): f(j)

    bar=pltpu.get_barrier_semaphore()
    loop(NR,lambda j: pl.semaphore_signal(bar,inc=1,device_id=(rp_(j),col),device_id_type=MESH))
    loop(NC,lambda j: pl.semaphore_signal(bar,inc=1,device_id=(row,cp_(j)),device_id_type=MESH))
    pl.semaphore_wait(bar,NR-1+NC-1)

    Q=NB//NY; PC=Q//NY
    def nx(v,d): return jnp.bitwise_and(v+d,NY-1)
    def half(h): return slice(0,H) if h==0 else slice(H,2*H)
    def ab(h): return (z,y) if h==0 else (y,z)
    def dev(h,a,b): return a*NY+b if h==0 else b*NY+a
    def qref(ref,h,a): return ref.at[rows(a,Q),half(h)]
    def tq(i,h,a): return Traw.at[i,rows(a,Q),half(h)]
    def s1(i,h,d):
        a,b=ab(h); a2=nx(a,d)
        return rc(qref(mat,h,a2),tq(i,h,a2),s1s.at[h],s1r.at[i,h],row=dev(h,a2,b))
    def s1l(i,h):
        a,b=ab(h); return pltpu.make_async_copy(qref(mat,h,a),tq(i,h,a),loc.at[1+h])
    def scatter(i):
        @pl.when(row==i)
        def _():
            for h in range(2):
                s1l(i,h).start(); loop(NY,lambda d: s1(i,h,d).start())
    def p1(b,j):
        c=cp_(j); return rc(mat.at[rows(c,CP),0:NB],corner.at[b,rows(c,CP)],p1s.at[0],p1r.at[b%2],col=c)
    def p1w(b):
        pl.when(col!=b%2)(lambda: p1(b,1).wait_recv())
    for i in range(2):
        for jj in range(2):
            @pl.when((row==i)&(col==jj))
            def _(b=2*i+jj):
                cc=pltpu.make_async_copy(mat.at[rows(col,CP),0:NB],corner.at[b,rows(col,CP)],loc.at[0])
                cc.start()
                loop(NC,lambda j: p1(b,j).start())
                cc.wait()
    scatter(1)
    mine=rows(col,CP)
    def p2(n,j):
        r=(corner.at[0,mine],corner.at[1,mine],corner.at[2:4,mine])[n]
        return rc(r,r,p2s.at[n],p2r.at[n],row=rp_(j))
    def c3(j): return rc(corner.at[0,mine],corner.at[0,mine],c3s.at[0],c3r.at[0],col=cp_(j))
    def d3(j): return rc(corner.at[1:4,mine],corner.at[1:4,mine],d3s.at[0],d3r.at[0],col=cp_(j))
    G=(NC-1)*CP
    def c3w(): took(corner.at[0,0:G],c3r.at[0])
    def d3w(): took(corner.at[1:4,0:G],d3r.at[0])
    @pl.when(row==0)
    def _():
        p1w(0); loop(NR,lambda j: p2(0,j).start())
    @pl.when(row!=0)
    def _(): p2(0,1).wait_recv()
    loop(NC,lambda j: c3(j).start())

    def ls(i,j):
        k=cp_(j); return rc(mat.at[rows(k,PL),0:NB],Lraw.at[i,rows(k,PL)],lss.at[0],lsr.at[i],col=k)
    def ll(i): return pltpu.make_async_copy(mat.at[rows(col,PL),0:NB],Lraw.at[i,rows(col,PL)],loc.at[3])
    def lg(i,j):
        k=cp_(j); return rc(Lraw.at[i,rows(col,PL)],Lraw.at[i,rows(col,PL)],lgs.at[i],lgr.at[i],col=k)
    GL=(NC-1)*PL
    def lgw(i): took(Lraw.at[i,0:GL],lgr.at[i])
    def left_gather():
        for i in range(2):
            pl.when(col==i)(lambda: ll(i).wait())
            pl.when(col!=i)(lambda: ls(i,1).wait_recv())
            loop(NC,lambda j: lg(i,j).start())

    def src_ab(h,i): return (0,i) if h==0 else (i,0)
    def tp(i,h,a,b): return Traw.at[i,rows(a*NY+b,PC),half(h)]
    def s2(i,h,d):
        a,b=ab(h); b2=nx(b,d)
        return rc(tp(i,h,a,b2),tp(i,h,a,b2),s2s.at[i,h],s2r.at[i,h],row=dev(h,a,b2))
    def g1(i,h,d,ss):
        a,b=ab(h); b2=nx(b,d)
        return rc(tp(i,h,a,b),tp(i,h,a,b),ss.at[i,h],g1r.at[i,h],row=dev(h,a,b2))
    def tt(i,h,n): return Traw.at[i,0:n,half(h)]
    def g1w(i,h): took(tt(i,h,3*PC),g1r.at[i,h])
    def g2(i,h,d):
        a,b=ab(h)
        return rc(tq(i,h,a),tq(i,h,a),g2s.at[i,h],g2r.at[i,h],row=dev(h,nx(a,d),b))
    def g3(i,h,d):
        a,b=ab(h); r=Traw.at[i,pl.ds(pl.multiple_of(nx(a,NY-d)*Q+(0 if d==1 else Q//2),Q//2),Q//2),half(h)]
        return rc(r,r,g3s.at[i,h],g3r.at[i,h],row=dev(h,nx(a,d),b))
    def g3w(i,h): took(tt(i,h,Q),g3r.at[i,h])
    each=[(i,h) for i in range(2) for h in range(2)]
    def inner_is_src(i,h): return ab(h)[1]==src_ab(h,i)[1]
    def top_s2(n):
        for i,h in each:
            if i!=n: continue
            @pl.when(inner_is_src(i,h))
            def _(i=i,h=h):
                pl.when(row==i)(lambda: s1l(i,h).wait())
                pl.when(row!=i)(lambda: s1(i,h,1).wait_recv())
                def f(d):
                    s2(i,h,d).start(); g1(i,h,d,s2p).start()
                loop(NY,f)
    def top_g1(n):
        for i,h in each:
            if i!=n: continue
            sb=src_ab(h,i)[1]; b=ab(h)[1]
            @pl.when(b!=sb)
            def _(i=i,h=h,sb=sb,b=b):
                s2(i,h,1).wait_recv()
                loop(NY,lambda d: pl.when(nx(b,d)!=sb)(lambda: g1(i,h,d,g1s).start()))
    def top_g2(n):
        for i,h in each:
            if i!=n: continue
            @pl.when(ab(h)[1]!=src_ab(h,i)[1])
            def _(i=i,h=h): g1w(i,h)
            for d in (1,NY-1): g2(i,h,d).start()

    for i in range(2):
        if i==0: scatter(0)
        @pl.when(col==i)
        def _(i=i):
            ll(i).start(); loop(NC,lambda j: ls(i,j).start())
    @pl.when(row==0)
    def _():
        p1w(1); loop(NR,lambda j: p2(1,j).start())
    @pl.when(row==1)
    def _():
        p1w(2); p1w(3); loop(NR,lambda j: p2(2,j).start())
    c3w()
    def rest_corners():
        pl.when(row!=0)(lambda: p2(1,1).wait_recv())
        pl.when(row!=1)(lambda: p2(2,1).wait_recv())
        loop(NC,lambda j: d3(j).start())

    def dump(li,ut):
        for ref,src in ((li,LI),(ut,UT)):
            for n,x in enumerate(split2(src[...])): ref[n]=x
    def top_g3(n):
        for h in range(2):
            took(tt(n,h,2*Q),g2r.at[n,h])
            for d in (1,NY-1): g3(n,h,d).start()
    def drain():
        for i in range(2):
            pl.when((row==i)&(col<2))(lambda: took(corner.at[0,0:G],p1s.at[0]))
            pl.when(col==i)(lambda: took(Lraw.at[0,0:GL],lss.at[0]))
        @pl.when(row==0)
        def _():
            for n in range(2): took(Lraw.at[0,0:(NR-1)*CP],p2s.at[n])
        pl.when(row==1)(lambda: took(Lraw.at[0,0:2*(NR-1)*CP],p2s.at[2]))
        took(corner.at[0,0:G],c3s.at[0]); took(corner.at[1:4,0:G],d3s.at[0])
        for i,h in each:
            b=ab(h)[1]; sb=src_ab(h,i)[1]
            pl.when(row==i)(lambda: took(tt(0,h,3*Q),s1s.at[h]))
            @pl.when(b==sb)
            def _(i=i,h=h):
                took(tt(0,h,3*PC),s2s.at[i,h]); took(tt(0,h,3*PC),s2p.at[i,h])
            pl.when(b!=sb)(lambda: took(tt(0,h,2*PC),g1s.at[i,h]))
    acts=[(AT["d3"][0],rest_corners),(AT["lg"][0],left_gather)]
    for f,n in ((top_s2,"s2"),(top_g1,"g1"),(top_g2,"g2"),(top_g3,"g3")):
        acts+=[(AT[n][k],functools.partial(f,k)) for k in (0,1)]
    lu_inv(corner[0],W,V,U,LT,LI,UT,[x for x in acts if x[0]<8])
    finish(U,LT,pk0); dump(li0,ut0)
    d3w()
    L=sum(dotT(corner[2],ut0[n]) for n in (1,0)).astype(BF)
    T=sum(jnp.dot(li0[n],corner[1],preferred_element_type=F) for n in (1,0)).astype(BF)
    l10[...]=L; t01[...]=T
    a=(corner[3].astype(F)-jnp.dot(L,T,preferred_element_type=F)).astype(BF)
    lu_inv(a,W,V,U,LT,LI,UT,[(x[0]-8,x[1]) for x in acts if x[0]>=8])
    finish(U,LT,pk1); dump(li1,ut1)
    drain()
    for i in range(2):
        lgw(i)
    def mm(x,y): return jnp.dot(x,y,preferred_element_type=F)
    LB=NB
    def lsolve(k,_):
        w=pl.ds(pl.multiple_of(k*LB,LB),LB)
        x=Lraw[0,w]
        x=(dotT(x,ut0[1])+dotT(x,ut0[0])).astype(BF)
        Lout[0,w]=x
        x=(Lraw[1,w].astype(F)-mm(x,t01[...])).astype(BF)
        Lout[1,w]=(dotT(x,ut1[1])+dotT(x,ut1[0])).astype(BF)
        return 0
    lax.fori_loop(0,mat.shape[0]//LB,lsolve,0,unroll=True)
    TB=cols//7
    for i,h in each:
        if i==0: g3w(i,h)
    def tsolve0(k,_):
        w=pl.ds(pl.multiple_of(k*TB,TB),TB)
        x=Traw[0,:,w]
        Tout[0,:,w]=(mm(li0[1],x)+mm(li0[0],x)).astype(BF)
        return 0
    lax.fori_loop(0,7,tsolve0,0,unroll=True)
    for i,h in each:
        if i==1: g3w(i,h)
    def tsolve1(k,_):
        w=pl.ds(pl.multiple_of(k*TB,TB),TB)
        x=(Traw[1,:,w].astype(F)-mm(l10[...],Tout[0,:,w])).astype(BF)
        Tout[1,:,w]=(mm(li1[1],x)+mm(li1[0],x)).astype(BF)
        return 0
    lax.fori_loop(0,7,tsolve1,0,unroll=True)
    for i in range(2): took(Lraw.at[i,0:GL],lgs.at[i])
    for i,h in each:
        took(tt(i,h,2*Q),g2s.at[i,h]); took(tt(i,h,Q),g3s.at[i,h])

def front(mat):
    rows_,cols_=mat.shape
    vm=pl.BlockSpec(memory_space=pltpu.VMEM); an=pl.BlockSpec(memory_space=pl.ANY)
    s=jax.ShapeDtypeStruct((NB,NB),BF)
    dma=pltpu.SemaphoreType.DMA
    return pl.pallas_call(front_kernel,
        out_shape=[jax.ShapeDtypeStruct((2,rows_,NB),BF),jax.ShapeDtypeStruct((2,NB,cols_),BF),s,s],
        in_specs=[an],out_specs=[vm]*4,
        scratch_shapes=[pltpu.VMEM((2,rows_,NB),BF),pltpu.VMEM((2,NB,cols_),BF)]+[pltpu.VMEM((2,NB,NB),BF)]*4+[pltpu.VMEM((NB,NB),BF)]*2+[pltpu.VMEM((4,NB,NB),BF)]+[pltpu.VMEM((NB,NB),F)]*6+[
            dma((1,)),dma((2,)),dma((3,)),dma((3,)),dma((1,)),dma((1,)),dma((1,)),dma((1,)),
            dma((1,)),dma((2,)),dma((2,)),dma((2,)),
            dma((2,)),dma((2,2)),dma((2,2)),dma((2,2)),dma((2,2)),dma((2,2)),dma((2,2)),dma((2,2)),dma((2,2)),dma((2,2)),dma((2,2)),dma((4,))],
        compiler_params=pltpu.CompilerParams(collective_id=0,has_side_effects=True,vmem_limit_bytes=40*2**20))(mat)

def update_kernel(a, L, T, pk0, pk1, out):
    t=pl.program_id(0)
    row=lax.axis_index("row"); col=lax.axis_index("col")
    def mm(x,y): return jnp.dot(x,y,preferred_element_type=F)
    for r in range(a.shape[0]//NB):
        w=pl.ds(r*NB,NB)
        y=(a[w].astype(F)-mm(L[0,w],T[0])).astype(BF)
        out[w]=(y.astype(F)-mm(L[1,w],T[1])).astype(BF)
    for c in range(2):
        @pl.when((t==0)&(col==c))
        def _(c=c): out[:,0:NB]=L[c]
    @pl.when(row==0)
    def _():
        out[0:NB]=T[0]
        @pl.when((t==0)&(col==0))
        def _(): out[0:NB,0:NB]=pk0[...]
    @pl.when(row==1)
    def _():
        out[0:NB,NB:]=T[1,:,NB:]
        @pl.when((t>0)|(col>1))
        def _(): out[0:NB,0:NB]=T[1,:,0:NB]
        @pl.when((t==0)&(col==1))
        def _(): out[0:NB,0:NB]=pk1[...]

CW=512

def update(mat, L, T, pk0, pk1):
    rows_,cols_=mat.shape
    vm=pl.BlockSpec(memory_space=pltpu.VMEM)
    return pl.pallas_call(update_kernel,grid=(cols_//CW,),
        out_shape=jax.ShapeDtypeStruct(mat.shape,BF),
        in_specs=[pl.BlockSpec((rows_,CW),lambda t:(0,t)),vm,pl.BlockSpec((2,NB,CW),lambda t:(0,0,t)),vm,vm],
        out_specs=pl.BlockSpec((rows_,CW),lambda t:(0,t)),
        compiler_params=pltpu.CompilerParams(vmem_limit_bytes=40*2**20))(mat,L,T,pk0,pk1)

def on_device(mat):
    return update(mat,*front(mat))

def solution(mesh):
    return jax.shard_map(on_device,mesh=mesh,in_specs=(P("row","col"),),out_specs=P("row","col"),check_vma=False)
```
